32 devices in a mesh: row: 4 (over z), col: 8 (over y, x, core).
Axes of the slice: x: 2, y: 2, z: 4, core: 2. Of those that a mesh axis runs over, the one named last changes fastest.
Arguments:
- amplitudes: bfloat16 [8, 1024, 3072], P('row', None, 'col'), may hold values from -6 to 6
- integrals: bfloat16 [32, 1024, 1024], P('row', 'col'), may hold values from -0.1875 to 0.1875
- source_pair: int32 [32], P('row'), may hold values from 0 to 7, as said below
- target_pair: int32 [32], P('row'), may hold values from 0 to 1
- symmetry_mask: int32 [32], P('row'), may hold values from 0 to 1
Outputs:
- residual: float32 [8, 1024, 3072], P('row', None, 'col')
The draws below stay inside these ranges and needn't reach their ends.
Inputs may be any that keep to these rules, and one draw needn't show every extreme that they name: The tile pairs owned by one owner group (source_pair // 2) are named by exactly 2 of the 8 slots of every owner group, and, for every position j, the 8 slots at position j within their owner groups (one per owner group) name each owner group's tile pairs exactly once.
All inputs are finite; a program needn't handle non-finite values.
Results may differ from the reference program's by a relative error of at most 0.0029.
Values may be sent and summed in bfloat16 or wider, within the bound.
A program may use at most 128 MiB of HBM per device.

```python
import jax
import jax.numpy as jnp
from jax import lax

TILE2 = 1024
PAIR_ROW = 2
TASK_ROW = 8
OCC = 3072
NPAIR = 8
NTASK = 32


def draw_source_pair(key, part):
    key = jax.random.fold_in(key, 11)
    first, second, third = jax.random.split(key, 3)
    groups = NTASK // TASK_ROW
    group_shift = jax.random.permutation(first, groups).astype(jnp.int32)
    slot_shift = jax.random.permutation(second, TASK_ROW).astype(jnp.int32)
    owner_group = (group_shift[:, None] + slot_shift[None, :]) % groups
    within = jax.random.randint(third, (groups, TASK_ROW), 0, PAIR_ROW).astype(jnp.int32)
    return (owner_group * PAIR_ROW + within).astype(jnp.int32).reshape(NTASK)


def draw_symmetry_mask(key, part):
    key = jax.random.fold_in(key, 7)
    first, second = jax.random.split(key)
    groups = NTASK // TASK_ROW
    level = jax.random.permutation(first, groups)
    limit = (level + 1) * (level + 1)
    rolls = jax.random.randint(second, (groups, TASK_ROW), 0, groups * groups)
    return (rolls < limit[:, None]).astype(jnp.int32).reshape(NTASK)


def plant(drawn, rng, low, top_value):
    longest = drawn.shape.index(max(drawn.shape))
    spots = []
    for shift in (0, 1):
        where = [jax.random.randint(jax.random.fold_in(rng, axis), (), 0, length) for axis, length in enumerate(drawn.shape)]
        where[longest] = (where[longest] + shift) % drawn.shape[longest]
        spots.append(tuple(where))
    return drawn.at[spots[0]].set(low).at[spots[1]].set(top_value)


def steps_of(rng, extent, shards, low, top_value):
    loudness = 1.0
    for dim, parts in shards:
        steps = jax.random.uniform(jax.random.fold_in(jax.random.fold_in(rng, 6), dim), (parts,), jnp.float32, low / len(shards), top_value / len(shards))
        loudness = loudness * jnp.repeat(jnp.exp(steps), extent[dim] // parts).reshape((-1,) + (1,) * (len(extent) - 1 - dim))
    return loudness


def noise(own_key, shape, spread, most, cuts=(), kind=jnp.bfloat16):
    array = spread * jax.random.normal(own_key, shape, jnp.float32)
    if cuts:
        array = array * steps_of(own_key, shape, cuts, -0.22, 0.18)
    return jnp.clip(array, -most, most).astype(kind)


def setup_inputs(seed: int = 0) -> dict:
    arg_keys = jax.random.split(jax.random.key(seed), 6)
    amplitudes = noise(arg_keys[0], (NPAIR, TILE2, OCC), 1.0, 6.0, ((0, 4), (2, 8)))
    integrals = noise(arg_keys[1], (NTASK, TILE2, TILE2), TILE2 ** -0.5, 0.1875, ((0, 4), (1, 8)))
    source_pair = draw_source_pair(jax.random.fold_in(arg_keys[5], 71), 0)
    target_pair = plant(jax.random.randint(arg_keys[3], (NTASK,), 0, PAIR_ROW), jax.random.fold_in(arg_keys[3], 1), 0, PAIR_ROW - 1).astype(jnp.int32)
    symmetry_mask = draw_symmetry_mask(jax.random.fold_in(arg_keys[5], 71), 0)
    return dict(amplitudes=amplitudes, integrals=integrals, source_pair=source_pair, target_pair=target_pair, symmetry_mask=symmetry_mask)


def reference(amplitudes, integrals, source_pair, target_pair, symmetry_mask):
    owner = jnp.arange(NTASK, dtype=jnp.int32) // TASK_ROW
    global_target = (owner * PAIR_ROW + target_pair).astype(jnp.int32)

    def step(total, item):
        tile_rows, source, target, allowed = item
        tile = lax.dynamic_index_in_dim(amplitudes, source.astype(jnp.int32), 0, keepdims=False)
        product = jnp.dot(tile_rows, tile, preferred_element_type=jnp.float32).astype(jnp.bfloat16)
        product = lax.optimization_barrier(product).astype(jnp.float32)
        current = lax.dynamic_index_in_dim(total, target, 0, keepdims=False)
        updated = current + jnp.where(allowed > 0, product, jnp.zeros_like(product))
        return lax.dynamic_update_index_in_dim(total, updated, target, 0), None

    start = jnp.zeros((NPAIR, TILE2, OCC), jnp.float32)
    total, unused = lax.scan(step, start, (integrals, source_pair, global_target, symmetry_mask))
    return total
```

```python
import functools

import jax
import jax.numpy as jnp
from jax import lax
from jax.experimental import pallas as pl
from jax.experimental.pallas import tpu as pltpu
from jax.sharding import PartitionSpec as P

MESH = pl.DeviceIdType.MESH
CHUNKS = 4
ROW_TILE = 256


def line_kernel(groups, source, target, mask, amp, integ, out, table, own, u1, u2, u3, d1, d2, d3,
                local_sem, isend, irecv, usend, urecv, dsend, drecv):
    z = lax.axis_index("row")
    col = lax.axis_index("col")
    core, x, y = col % 2, (col // 2) % 2, col // 4
    slots, rows, _ = integ.shape
    half = slots // 2
    pairs, depth, _ = amp.shape

    def place(py, px, pc):
        return (py * 2 + px) * 2 + pc

    sib, xn, yn = place(y, x, 1 - core), place(y, 1 - x, core), place(1 - y, x, core)
    diag = place(1 - y, 1 - x, core)
    low, high = z > 0, z < groups - 1

    barrier = pltpu.get_barrier_semaphore()
    for partner in (sib, xn, yn):
        pl.semaphore_signal(barrier, inc=1, device_id=(z, partner), device_id_type=MESH)

    @pl.when(low)
    def _():
        pl.semaphore_signal(barrier, inc=1, device_id=(z - 1, col), device_id_type=MESH)

    @pl.when(high)
    def _():
        pl.semaphore_signal(barrier, inc=1, device_id=(z + 1, col), device_id_type=MESH)

    own_rows = table.at[:, pl.ds(col * rows, rows), :]
    fetch_i = pltpu.make_async_copy(integ, own_rows, local_sem.at[0])
    fetch_a = pltpu.make_async_copy(amp, own, local_sem.at[1])
    fetch_i.start()
    fetch_a.start()
    pl.semaphore_wait(barrier, 3 + jnp.where(low, 1, 0) + jnp.where(high, 1, 0))

    per_tile = CHUNKS // pairs
    chunk_rows = depth // per_tile

    def piece(ref, q):
        return ref.at[q // per_tile, pl.ds((q % per_tile) * chunk_rows, chunk_rows), :]

    ups, downs = (own, u1, u2, u3), (own, d1, d2, d3)

    def up(d, q):
        src = amp if d == 1 else ups[d - 1]
        i = (d - 1) * CHUNKS + q
        return pltpu.make_async_remote_copy(
            piece(src, q), piece(ups[d], q), usend.at[i], urecv.at[i],
            device_id=(z + 1, col), device_id_type=MESH)

    def down(d, q):
        src = amp if d == 1 else downs[d - 1]
        i = (d - 1) * CHUNKS + q
        return pltpu.make_async_remote_copy(
            piece(src, q), piece(downs[d], q), dsend.at[i], drecv.at[i],
            device_id=(z - 1, col), device_id_type=MESH)

    def rows_copy(i, block, first, count, partner):
        window = table.at[pl.ds(first, count), pl.ds(block * rows, rows), :]
        src = integ.at[pl.ds(first, count)] if i < 5 else window
        return pltpu.make_async_remote_copy(
            src, window, isend.at[i], irecv.at[i], device_id=(z, partner), device_id_type=MESH)

    moves = [
        rows_copy(0, col, 0, slots, sib),
        rows_copy(1, col, half, half, xn),
        rows_copy(2, col, 0, half, xn),
        rows_copy(3, col, 0, half, yn),
        rows_copy(4, col, half, half, yn),
        rows_copy(5, yn, 0, half, xn),
        rows_copy(6, xn, half, half, yn),
        rows_copy(7, xn, half, half, sib),
        rows_copy(8, xn, 0, half, sib),
        rows_copy(9, yn, 0, half, sib),
        rows_copy(10, yn, half, half, sib),
        rows_copy(11, diag, 0, half, sib),
        rows_copy(12, diag, half, half, sib),
    ]

    for q in range(CHUNKS):
        @pl.when(low)
        def _():
            down(1, q).start()

        @pl.when(high)
        def _():
            up(1, q).start()

    for i in (1, 3, 2, 4, 0):
        moves[i].start()

    def pass_on(d, q):
        @pl.when(z >= d)
        def _():
            up(d, q).wait_recv()
            if d < groups - 1:
                @pl.when(high)
                def _():
                    up(d + 1, q).start()

        @pl.when(z + d < groups)
        def _():
            down(d, q).wait_recv()
            if d < groups - 1:
                @pl.when(low)
                def _():
                    down(d + 1, q).start()

    out[...] = jnp.zeros_like(out)
    mid = CHUNKS // 2
    for q in range(mid):
        pass_on(1, q)
    moves[3].wait_recv()
    moves[5].start()
    moves[9].start()
    moves[1].wait_recv()
    moves[6].start()
    moves[7].start()
    for q in range(mid, CHUNKS):
        pass_on(1, q)
    moves[4].wait_recv()
    moves[10].start()
    moves[2].wait_recv()
    moves[8].start()
    for q in range(mid):
        pass_on(2, q)
    moves[5].wait_recv()
    moves[11].start()
    moves[6].wait_recv()
    moves[12].start()
    for q in range(mid, CHUNKS):
        pass_on(2, q)
    fetch_i.wait()
    fetch_a.wait()
    for i in (0, 7, 8, 9, 10, 11, 12):
        moves[i].wait_recv()

    def contract(tiles, group):
        first = jnp.int32(slots)
        last = jnp.int32(-1)
        for k in range(slots):
            match = source[k] // pairs == group
            first = jnp.where(match, jnp.minimum(first, k), first)
            last = jnp.where(match, jnp.maximum(last, k), last)
        for k in (first, last):
            k = jnp.clip(k, 0, slots - 1)
            tile = source[k] % pairs
            goal = jnp.where(mask[k] > 0, target[k], -1)

            @pl.loop(0, depth // ROW_TILE)
            def _(r):
                span = pl.ds(pl.multiple_of(r * ROW_TILE, ROW_TILE), ROW_TILE)
                product = jnp.dot(table[k, span, :], tiles[tile], preferred_element_type=jnp.float32)
                product = product.astype(jnp.bfloat16).astype(jnp.float32)
                for p in range(pairs):
                    out[p, span, :] += jnp.where(goal == p, product, 0.0)

    contract(own, z)
    for d in range(1, groups):
        if d == groups - 1:
            for q in range(CHUNKS):
                pass_on(d, q)

        @pl.when(z >= d)
        def _():
            contract(ups[d], z - d)

        @pl.when(z + d < groups)
        def _():
            contract(downs[d], z + d)

    for move in moves:
        move.wait_send()
    for d in range(1, groups):
        for q in range(CHUNKS):
            @pl.when(high & (z >= d - 1))
            def _():
                up(d, q).wait_send()

            @pl.when(low & (z + d - 1 < groups))
            def _():
                down(d, q).wait_send()


def on_line(groups, amplitudes, integrals, source_pair, target_pair, symmetry_mask):
    pairs, depth, width = amplitudes.shape
    slots, rows, inner = integrals.shape
    across = depth // rows
    shard = pltpu.VMEM(amplitudes.shape, amplitudes.dtype)
    hops = (groups - 1) * CHUNKS
    return pl.pallas_call(
        functools.partial(line_kernel, groups),
        out_shape=jax.ShapeDtypeStruct((pairs, depth, width), jnp.float32),
        in_specs=[pl.BlockSpec(memory_space=pltpu.SMEM)] * 3 + [pl.BlockSpec(memory_space=pl.ANY)] * 2,
        out_specs=pl.BlockSpec(memory_space=pltpu.VMEM),
        scratch_shapes=[
            pltpu.VMEM((slots, rows * across, inner), integrals.dtype),
            shard, shard, shard, shard, shard, shard, shard,
            pltpu.SemaphoreType.DMA((2,)),
            pltpu.SemaphoreType.DMA((13,)),
            pltpu.SemaphoreType.DMA((13,)),
            pltpu.SemaphoreType.DMA((hops,)),
            pltpu.SemaphoreType.DMA((hops,)),
            pltpu.SemaphoreType.DMA((hops,)),
            pltpu.SemaphoreType.DMA((hops,)),
        ],
        compiler_params=pltpu.CompilerParams(
            collective_id=0, has_side_effects=True, vmem_limit_bytes=48 * 1024 * 1024
        ),
        cost_estimate=pl.CostEstimate(
            flops=2 * slots * depth * inner * width, bytes_accessed=16 * 1024 * 1024, transcendentals=0
        ),
    )(source_pair, target_pair, symmetry_mask, amplitudes, integrals)


def on_device(amplitudes, integrals, source_pair, target_pair, symmetry_mask):
    pairs = amplitudes.shape[0]
    tile_table = lax.all_gather(amplitudes, "row", axis=0, tiled=True)
    piece = lax.all_gather(integrals, "col", axis=1, tiled=True)
    total = [jnp.zeros(amplitudes.shape[1:], jnp.float32)] * pairs
    for slot in range(integrals.shape[0]):
        tile = lax.dynamic_index_in_dim(tile_table, source_pair[slot], 0, keepdims=False)
        product = jnp.dot(piece[slot], tile, preferred_element_type=jnp.float32).astype(jnp.bfloat16)
        goal = jnp.where(symmetry_mask[slot] > 0, target_pair[slot], -1)
        for p in range(pairs):
            total[p] += jnp.where(goal == p, product.astype(jnp.float32), 0.0)
    return jnp.stack(total)


def solution(mesh):
    placed = (P("row", None, "col"), P("row", "col", None), P("row"), P("row"), P("row"))
    groups = mesh.shape["row"]
    if groups == 4 and mesh.shape["col"] == 8:
        body = functools.partial(on_line, groups)
    else:
        body = on_device
    return jax.shard_map(
        body, mesh=mesh, in_specs=placed, out_specs=P("row", None, "col"), check_vma=False
    )
```

```python
import functools

import jax
import jax.numpy as jnp
from jax import lax
from jax.experimental import pallas as pl
from jax.experimental.pallas import tpu as pltpu
from jax.sharding import PartitionSpec as P

MESH = pl.DeviceIdType.MESH
CHUNKS = 4
ROW_TILE = 256


def line_kernel(groups, source_hbm, target_hbm, mask_hbm, amp, integ, out, source, target, mask, table, own,
                u1, u2, d1, d2, far_head, far_tail, part, scalar_sem,
                local_sem, isend, irecv, usend, urecv, dsend, drecv):
    z = lax.axis_index("row")
    col = lax.axis_index("col")
    core, x, y = col % 2, (col // 2) % 2, col // 4
    slots, rows, _ = integ.shape
    half = slots // 2
    pairs, depth, _ = amp.shape

    def place(py, px, pc):
        return (py * 2 + px) * 2 + pc

    sib, xn, yn = place(y, x, 1 - core), place(y, 1 - x, core), place(1 - y, x, core)
    diag = place(1 - y, 1 - x, core)
    low, high = z > 0, z < groups - 1

    barrier = pltpu.get_barrier_semaphore()
    for partner in (sib, xn, yn):
        pl.semaphore_signal(barrier, inc=1, device_id=(z, partner), device_id_type=MESH)

    @pl.when(low)
    def _():
        pl.semaphore_signal(barrier, inc=1, device_id=(z - 1, col), device_id_type=MESH)

    @pl.when(high)
    def _():
        pl.semaphore_signal(barrier, inc=1, device_id=(z + 1, col), device_id_type=MESH)

    own_rows = table.at[:, pl.ds(col * rows, rows), :]
    fetch_i = pltpu.make_async_copy(integ, own_rows, local_sem.at[0])
    fetch_a = pltpu.make_async_copy(amp, own, local_sem.at[1])
    scalars = [
        pltpu.make_async_copy(src, dst, scalar_sem.at[i])
        for i, (src, dst) in enumerate(((source_hbm, source), (target_hbm, target), (mask_hbm, mask)))
    ]
    fetch_i.start()
    fetch_a.start()
    for scalar in scalars:
        scalar.start()
    pl.semaphore_wait(barrier, 3 + jnp.where(low, 1, 0) + jnp.where(high, 1, 0))

    chunk_rows = depth // CHUNKS

    def piece(ref, q):
        if ref is None:
            if q == CHUNKS - 1:
                return far_tail
            ref = far_head
        return ref.at[:, pl.ds(q * chunk_rows, chunk_rows), :]

    ups, downs = (own, u1, u2, None), (own, d1, d2, None)

    def up(d, q):
        src = amp if d == 1 else ups[d - 1]
        i = (d - 1) * CHUNKS + q
        return pltpu.make_async_remote_copy(
            piece(src, q), piece(ups[d], q), usend.at[i], urecv.at[i],
            device_id=(z + 1, col), device_id_type=MESH)

    def down(d, q):
        src = amp if d == 1 else downs[d - 1]
        i = (d - 1) * CHUNKS + q
        return pltpu.make_async_remote_copy(
            piece(src, q), piece(downs[d], q), dsend.at[i], drecv.at[i],
            device_id=(z - 1, col), device_id_type=MESH)

    def rows_copy(i, block, first, count, partner):
        window = table.at[pl.ds(first, count), pl.ds(block * rows, rows), :]
        src = integ.at[pl.ds(first, count)] if i < 5 else window
        return pltpu.make_async_remote_copy(
            src, window, isend.at[i], irecv.at[i], device_id=(z, partner), device_id_type=MESH)

    moves = [
        rows_copy(0, col, 0, slots, sib),
        rows_copy(1, col, half, half, xn),
        rows_copy(2, col, 0, half, xn),
        rows_copy(3, col, 0, half, yn),
        rows_copy(4, col, half, half, yn),
        rows_copy(5, yn, 0, half, xn),
        rows_copy(6, xn, half, half, yn),
        rows_copy(7, xn, half, half, sib),
        rows_copy(8, xn, 0, half, sib),
        rows_copy(9, yn, 0, half, sib),
        rows_copy(10, yn, half, half, sib),
        rows_copy(11, diag, 0, half, sib),
        rows_copy(12, diag, half, half, sib),
    ]

    for q in range(CHUNKS):
        @pl.when(low)
        def _():
            down(1, q).start()

        @pl.when(high)
        def _():
            up(1, q).start()

    for i in (1, 3, 2, 4, 0):
        moves[i].start()

    def pass_on(d, q):
        @pl.when(z >= d)
        def _():
            up(d, q).wait_recv()
            if d < groups - 1:
                @pl.when(high)
                def _():
                    up(d + 1, q).start()

        @pl.when(z + d < groups)
        def _():
            down(d, q).wait_recv()
            if d < groups - 1:
                @pl.when(low)
                def _():
                    down(d + 1, q).start()

    out[...] = jnp.zeros_like(out)
    mid = CHUNKS // 2
    for q in range(mid):
        pass_on(1, q)
    moves[3].wait_recv()
    moves[5].start()
    moves[9].start()
    moves[1].wait_recv()
    moves[6].start()
    moves[7].start()
    for q in range(mid, CHUNKS):
        pass_on(1, q)
    moves[4].wait_recv()
    moves[10].start()
    moves[2].wait_recv()
    moves[8].start()
    for q in range(mid):
        pass_on(2, q)
    moves[5].wait_recv()
    moves[11].start()
    moves[6].wait_recv()
    moves[12].start()
    for q in range(mid, CHUNKS):
        pass_on(2, q)
    fetch_i.wait()
    fetch_a.wait()
    for i in (0, 7, 8, 9, 10, 11, 12):
        moves[i].wait_recv()

    for scalar in scalars:
        scalar.wait()

    def slots_of(group):
        first = jnp.int32(slots)
        last = jnp.int32(-1)
        for k in range(slots):
            match = source[k] // pairs == group
            first = jnp.where(match, jnp.minimum(first, k), first)
            last = jnp.where(match, jnp.maximum(last, k), last)
        found = []
        for k in (first, last):
            k = jnp.clip(k, 0, slots - 1)
            found.append((k, source[k] % pairs, jnp.where(mask[k] > 0, target[k], -1)))
        return found

    def contract(tiles, group):
        for k, tile, goal in slots_of(group):

            @pl.loop(0, depth // ROW_TILE)
            def _(r):
                span = pl.ds(pl.multiple_of(r * ROW_TILE, ROW_TILE), ROW_TILE)
                product = jnp.dot(table[k, span, :], tiles[tile], preferred_element_type=jnp.float32)
                product = product.astype(jnp.bfloat16).astype(jnp.float32)
                for p in range(pairs):
                    out[p, span, :] += jnp.where(goal == p, product, 0.0)

    contract(own, z)
    for d in range(1, groups - 1):
        @pl.when(z >= d)
        def _():
            contract(ups[d], z - d)

        @pl.when(z + d < groups)
        def _():
            contract(downs[d], z + d)

    last_hop = groups - 1
    for q in range(CHUNKS - 1):
        pass_on(last_hop, q)
    head = depth - chunk_rows
    outer = (z == 0) | (z == groups - 1)

    @pl.when(outer)
    def _():
        for n, (k, tile, _) in enumerate(slots_of(groups - 1 - z)):
            @pl.loop(0, depth // ROW_TILE)
            def _(r):
                span = pl.ds(pl.multiple_of(r * ROW_TILE, ROW_TILE), ROW_TILE)
                part[n, span, :] = jnp.dot(
                    table[k, span, :head], far_head[tile], preferred_element_type=jnp.float32)

    pass_on(last_hop, CHUNKS - 1)

    @pl.when(outer)
    def _():
        found = slots_of(groups - 1 - z)
        for r in range(depth // ROW_TILE):
            span = slice(r * ROW_TILE, (r + 1) * ROW_TILE)
            totals = [out[p, span, :] for p in range(pairs)]
            for n, (k, tile, goal) in enumerate(found):
                product = part[n, span, :] + jnp.dot(
                    table[k, span, head:], far_tail[tile], preferred_element_type=jnp.float32)
                product = product.astype(jnp.bfloat16).astype(jnp.float32)
                totals = [total + jnp.where(goal == p, product, 0.0) for p, total in enumerate(totals)]
            for p in range(pairs):
                out[p, span, :] = totals[p]

    for move in moves:
        move.wait_send()
    for d in range(1, groups):
        for q in range(CHUNKS):
            @pl.when(high & (z >= d - 1))
            def _():
                up(d, q).wait_send()

            @pl.when(low & (z + d - 1 < groups))
            def _():
                down(d, q).wait_send()


def on_line(groups, amplitudes, integrals, source_pair, target_pair, symmetry_mask):
    pairs, depth, width = amplitudes.shape
    slots, rows, inner = integrals.shape
    across = depth // rows
    shard = pltpu.VMEM(amplitudes.shape, amplitudes.dtype)
    hops = (groups - 1) * CHUNKS
    return pl.pallas_call(
        functools.partial(line_kernel, groups),
        out_shape=pltpu.VMEM((pairs, depth, width), jnp.float32),
        in_specs=[pl.BlockSpec(memory_space=pltpu.HBM)] * 5,
        out_specs=pl.BlockSpec(memory_space=pltpu.VMEM),
        scratch_shapes=[
            pltpu.SMEM((slots,), jnp.int32),
            pltpu.SMEM((slots,), jnp.int32),
            pltpu.SMEM((slots,), jnp.int32),
            pltpu.VMEM((slots, rows * across, inner), integrals.dtype),
            shard, shard, shard, shard, shard,
            pltpu.VMEM((pairs, depth - depth // CHUNKS, width), amplitudes.dtype),
            pltpu.VMEM((pairs, depth // CHUNKS, width), amplitudes.dtype),
            pltpu.VMEM((2, depth, width), jnp.float32),
            pltpu.SemaphoreType.DMA((3,)),
            pltpu.SemaphoreType.DMA((2,)),
            pltpu.SemaphoreType.DMA((13,)),
            pltpu.SemaphoreType.DMA((13,)),
            pltpu.SemaphoreType.DMA((hops,)),
            pltpu.SemaphoreType.DMA((hops,)),
            pltpu.SemaphoreType.DMA((hops,)),
            pltpu.SemaphoreType.DMA((hops,)),
        ],
        compiler_params=pltpu.CompilerParams(
            collective_id=0, has_side_effects=True, vmem_limit_bytes=60 * 1024 * 1024
        ),
        cost_estimate=pl.CostEstimate(
            flops=2 * slots * depth * inner * width, bytes_accessed=16 * 1024 * 1024, transcendentals=0
        ),
    )(source_pair, target_pair, symmetry_mask, amplitudes, integrals)


def on_device(amplitudes, integrals, source_pair, target_pair, symmetry_mask):
    pairs = amplitudes.shape[0]
    tile_table = lax.all_gather(amplitudes, "row", axis=0, tiled=True)
    piece = lax.all_gather(integrals, "col", axis=1, tiled=True)
    total = [jnp.zeros(amplitudes.shape[1:], jnp.float32)] * pairs
    for slot in range(integrals.shape[0]):
        tile = lax.dynamic_index_in_dim(tile_table, source_pair[slot], 0, keepdims=False)
        product = jnp.dot(piece[slot], tile, preferred_element_type=jnp.float32).astype(jnp.bfloat16)
        goal = jnp.where(symmetry_mask[slot] > 0, target_pair[slot], -1)
        for p in range(pairs):
            total[p] += jnp.where(goal == p, product.astype(jnp.float32), 0.0)
    return jnp.stack(total)


def solution(mesh):
    placed = (P("row", None, "col"), P("row", "col", None), P("row"), P("row"), P("row"))
    groups = mesh.shape["row"]
    if groups == 4 and mesh.shape["col"] == 8:
        body = functools.partial(on_line, groups)
    else:
        body = on_device
    return jax.shard_map(
        body, mesh=mesh, in_specs=placed, out_specs=P("row", None, "col"), check_vma=False
    )
```

```python
import functools

import jax
import jax.numpy as jnp
from jax import lax
from jax.experimental import pallas as pl
from jax.experimental.pallas import tpu as pltpu
from jax.sharding import PartitionSpec as P

MESH = pl.DeviceIdType.MESH
CHUNKS = 4
IN_FLIGHT = 2
ROW_TILE = 256


def line_kernel(groups, source_hbm, target_hbm, mask_hbm, amp, integ, out, source, target, mask, table, own,
                u1, u2, d1, d2, far_head, far_tail, part, scalar_sem,
                local_sem, isend, irecv, usend, urecv, dsend, drecv):
    z = lax.axis_index("row")
    col = lax.axis_index("col")
    core, x, y = col % 2, (col // 2) % 2, col // 4
    slots, rows, _ = integ.shape
    half = slots // 2
    pairs, depth, _ = amp.shape

    def place(py, px, pc):
        return (py * 2 + px) * 2 + pc

    sib, xn, yn = place(y, x, 1 - core), place(y, 1 - x, core), place(1 - y, x, core)
    diag = place(1 - y, 1 - x, core)
    low, high = z > 0, z < groups - 1

    barrier = pltpu.get_barrier_semaphore()
    for partner in (sib, xn, yn):
        pl.semaphore_signal(barrier, inc=1, device_id=(z, partner), device_id_type=MESH)

    @pl.when(low)
    def _():
        pl.semaphore_signal(barrier, inc=1, device_id=(z - 1, col), device_id_type=MESH)

    @pl.when(high)
    def _():
        pl.semaphore_signal(barrier, inc=1, device_id=(z + 1, col), device_id_type=MESH)

    own_rows = table.at[:, pl.ds(col * rows, rows), :]
    fetch_i = pltpu.make_async_copy(integ, own_rows, local_sem.at[0])
    fetch_a = pltpu.make_async_copy(amp, own, local_sem.at[1])
    scalars = [
        pltpu.make_async_copy(src, dst, scalar_sem.at[i])
        for i, (src, dst) in enumerate(((source_hbm, source), (target_hbm, target), (mask_hbm, mask)))
    ]
    fetch_i.start()
    fetch_a.start()
    for scalar in scalars:
        scalar.start()
    pl.semaphore_wait(barrier, 3 + jnp.where(low, 1, 0) + jnp.where(high, 1, 0))

    chunk_rows = depth // CHUNKS

    def piece(ref, q):
        if ref is None:
            if q == CHUNKS - 1:
                return far_tail
            ref = far_head
        return ref.at[:, pl.ds(q * chunk_rows, chunk_rows), :]

    ups, downs = (own, u1, u2, None), (own, d1, d2, None)

    def up(d, q):
        src = amp if d == 1 else ups[d - 1]
        i = (d - 1) * CHUNKS + q
        return pltpu.make_async_remote_copy(
            piece(src, q), piece(ups[d], q), usend.at[i], urecv.at[i],
            device_id=(z + 1, col), device_id_type=MESH)

    def down(d, q):
        src = amp if d == 1 else downs[d - 1]
        i = (d - 1) * CHUNKS + q
        return pltpu.make_async_remote_copy(
            piece(src, q), piece(downs[d], q), dsend.at[i], drecv.at[i],
            device_id=(z - 1, col), device_id_type=MESH)

    def rows_copy(i, block, first, count, partner):
        window = table.at[pl.ds(first, count), pl.ds(block * rows, rows), :]
        src = integ.at[pl.ds(first, count)] if i < 5 else window
        return pltpu.make_async_remote_copy(
            src, window, isend.at[i], irecv.at[i], device_id=(z, partner), device_id_type=MESH)

    moves = [
        rows_copy(0, col, 0, slots, sib),
        rows_copy(1, col, half, half, xn),
        rows_copy(2, col, 0, half, xn),
        rows_copy(3, col, 0, half, yn),
        rows_copy(4, col, half, half, yn),
        rows_copy(5, yn, 0, half, xn),
        rows_copy(6, xn, half, half, yn),
        rows_copy(7, xn, half, half, sib),
        rows_copy(8, xn, 0, half, sib),
        rows_copy(9, yn, 0, half, sib),
        rows_copy(10, yn, half, half, sib),
        rows_copy(11, diag, 0, half, sib),
        rows_copy(12, diag, half, half, sib),
    ]

    for q in range(CHUNKS):
        @pl.when(low)
        def _():
            down(1, q).start()

        @pl.when(high)
        def _():
            up(1, q).start()

    for i in (1, 3, 2, 4, 0):
        moves[i].start()

    def pass_on(d, q):
        @pl.when(z >= d)
        def _():
            up(d, q).wait_recv()
            if d < groups - 1:
                @pl.when(high)
                def _():
                    if d + 1 == groups - 1 and q >= IN_FLIGHT:
                        up(d + 1, q - IN_FLIGHT).wait_send()
                    up(d + 1, q).start()

        @pl.when(z + d < groups)
        def _():
            down(d, q).wait_recv()
            if d < groups - 1:
                @pl.when(low)
                def _():
                    if d + 1 == groups - 1 and q >= IN_FLIGHT:
                        down(d + 1, q - IN_FLIGHT).wait_send()
                    down(d + 1, q).start()

    out[...] = jnp.zeros_like(out)
    mid = CHUNKS // 2
    for q in range(mid):
        pass_on(1, q)
    moves[3].wait_recv()
    moves[5].start()
    moves[9].start()
    moves[1].wait_recv()
    moves[6].start()
    moves[7].start()
    for q in range(mid, CHUNKS):
        pass_on(1, q)
    moves[4].wait_recv()
    moves[10].start()
    moves[2].wait_recv()
    moves[8].start()
    for q in range(mid):
        pass_on(2, q)
    moves[5].wait_recv()
    moves[11].start()
    moves[6].wait_recv()
    moves[12].start()
    fetch_i.wait()
    fetch_a.wait()
    for i in (0, 7, 8, 9, 10, 11, 12):
        moves[i].wait_recv()

    for scalar in scalars:
        scalar.wait()

    def slots_of(group):
        first = jnp.int32(slots)
        last = jnp.int32(-1)
        for k in range(slots):
            match = source[k] // pairs == group
            first = jnp.where(match, jnp.minimum(first, k), first)
            last = jnp.where(match, jnp.maximum(last, k), last)
        found = []
        for k in (first, last):
            k = jnp.clip(k, 0, slots - 1)
            found.append((k, source[k] % pairs, jnp.where(mask[k] > 0, target[k], -1)))
        return found

    def contract(tiles, group):
        for k, tile, goal in slots_of(group):

            @pl.loop(0, depth // ROW_TILE)
            def _(r):
                span = pl.ds(pl.multiple_of(r * ROW_TILE, ROW_TILE), ROW_TILE)
                product = jnp.dot(table[k, span, :], tiles[tile], preferred_element_type=jnp.float32)
                product = product.astype(jnp.bfloat16).astype(jnp.float32)
                for p in range(pairs):
                    out[p, span, :] += jnp.where(goal == p, product, 0.0)

    contract(own, z)
    pass_on(2, mid)
    for d in range(1, groups - 1):
        if d == 2:
            for q in range(mid + 1, CHUNKS):
                pass_on(2, q)

        @pl.when(z >= d)
        def _():
            contract(ups[d], z - d)

        @pl.when(z + d < groups)
        def _():
            contract(downs[d], z + d)

    last_hop = groups - 1
    for q in range(CHUNKS - 1):
        pass_on(last_hop, q)
    head = depth - chunk_rows
    outer = (z == 0) | (z == groups - 1)

    @pl.when(outer)
    def _():
        for n, (k, tile, _) in enumerate(slots_of(groups - 1 - z)):
            @pl.loop(0, depth // ROW_TILE)
            def _(r):
                span = pl.ds(pl.multiple_of(r * ROW_TILE, ROW_TILE), ROW_TILE)
                part[n, span, :] = jnp.dot(
                    table[k, span, :head], far_head[tile], preferred_element_type=jnp.float32)

    pass_on(last_hop, CHUNKS - 1)

    @pl.when(outer)
    def _():
        found = slots_of(groups - 1 - z)
        for r in range(depth // ROW_TILE):
            span = slice(r * ROW_TILE, (r + 1) * ROW_TILE)
            totals = [out[p, span, :] for p in range(pairs)]
            for n, (k, tile, goal) in enumerate(found):
                product = part[n, span, :] + jnp.dot(
                    table[k, span, head:], far_tail[tile], preferred_element_type=jnp.float32)
                product = product.astype(jnp.bfloat16).astype(jnp.float32)
                totals = [total + jnp.where(goal == p, product, 0.0) for p, total in enumerate(totals)]
            for p in range(pairs):
                out[p, span, :] = totals[p]

    for move in moves:
        move.wait_send()
    for d in range(1, groups):
        for q in range(CHUNKS - IN_FLIGHT if d == last_hop else 0, CHUNKS):
            @pl.when(high & (z >= d - 1))
            def _():
                up(d, q).wait_send()

            @pl.when(low & (z + d - 1 < groups))
            def _():
                down(d, q).wait_send()


def on_line(groups, amplitudes, integrals, source_pair, target_pair, symmetry_mask):
    pairs, depth, width = amplitudes.shape
    slots, rows, inner = integrals.shape
    across = depth // rows
    shard = pltpu.VMEM(amplitudes.shape, amplitudes.dtype)
    hops = (groups - 1) * CHUNKS
    return pl.pallas_call(
        functools.partial(line_kernel, groups),
        out_shape=pltpu.VMEM((pairs, depth, width), jnp.float32),
        in_specs=[pl.BlockSpec(memory_space=pltpu.HBM)] * 5,
        out_specs=pl.BlockSpec(memory_space=pltpu.VMEM),
        scratch_shapes=[
            pltpu.SMEM((slots,), jnp.int32),
            pltpu.SMEM((slots,), jnp.int32),
            pltpu.SMEM((slots,), jnp.int32),
            pltpu.VMEM((slots, rows * across, inner), integrals.dtype),
            shard, shard, shard, shard, shard,
            pltpu.VMEM((pairs, depth - depth // CHUNKS, width), amplitudes.dtype),
            pltpu.VMEM((pairs, depth // CHUNKS, width), amplitudes.dtype),
            pltpu.VMEM((2, depth, width), jnp.float32),
            pltpu.SemaphoreType.DMA((3,)),
            pltpu.SemaphoreType.DMA((2,)),
            pltpu.SemaphoreType.DMA((13,)),
            pltpu.SemaphoreType.DMA((13,)),
            pltpu.SemaphoreType.DMA((hops,)),
            pltpu.SemaphoreType.DMA((hops,)),
            pltpu.SemaphoreType.DMA((hops,)),
            pltpu.SemaphoreType.DMA((hops,)),
        ],
        compiler_params=pltpu.CompilerParams(
            collective_id=0, has_side_effects=True, vmem_limit_bytes=60 * 1024 * 1024
        ),
        cost_estimate=pl.CostEstimate(
            flops=2 * slots * depth * inner * width, bytes_accessed=16 * 1024 * 1024, transcendentals=0
        ),
    )(source_pair, target_pair, symmetry_mask, amplitudes, integrals)


def on_device(amplitudes, integrals, source_pair, target_pair, symmetry_mask):
    pairs = amplitudes.shape[0]
    tile_table = lax.all_gather(amplitudes, "row", axis=0, tiled=True)
    piece = lax.all_gather(integrals, "col", axis=1, tiled=True)
    total = [jnp.zeros(amplitudes.shape[1:], jnp.float32)] * pairs
    for slot in range(integrals.shape[0]):
        tile = lax.dynamic_index_in_dim(tile_table, source_pair[slot], 0, keepdims=False)
        product = jnp.dot(piece[slot], tile, preferred_element_type=jnp.float32).astype(jnp.bfloat16)
        goal = jnp.where(symmetry_mask[slot] > 0, target_pair[slot], -1)
        for p in range(pairs):
            total[p] += jnp.where(goal == p, product.astype(jnp.float32), 0.0)
    return jnp.stack(total)


def solution(mesh):
    placed = (P("row", None, "col"), P("row", "col", None), P("row"), P("row"), P("row"))
    groups = mesh.shape["row"]
    if groups == 4 and mesh.shape["col"] == 8:
        body = functools.partial(on_line, groups)
    else:
        body = on_device
    return jax.shard_map(
        body, mesh=mesh, in_specs=placed, out_specs=P("row", None, "col"), check_vma=False
    )
```

```python
import functools

import jax
import jax.numpy as jnp
from jax import lax
from jax.experimental import pallas as pl
from jax.experimental.pallas import tpu as pltpu
from jax.sharding import PartitionSpec as P

MESH = pl.DeviceIdType.MESH
CHUNKS = 4
TAIL_SHARE = 8
ROW_TILE = 256


def line_kernel(groups, source_hbm, target_hbm, mask_hbm, amp, integ, out, source, target, mask, table, own,
                u1, u2, d1, d2, far_head, far_tail, picked, scalar_sem,
                local_sem, isend, irecv, usend, urecv, dsend, drecv):
    z = lax.axis_index("row")
    col = lax.axis_index("col")
    core, x, y = col % 2, (col // 2) % 2, col // 4
    slots, rows, _ = integ.shape
    half = slots // 2
    pairs, depth, _ = amp.shape

    def place(py, px, pc):
        return (py * 2 + px) * 2 + pc

    sib, xn, yn = place(y, x, 1 - core), place(y, 1 - x, core), place(1 - y, x, core)
    diag = place(1 - y, 1 - x, core)
    low, high = z > 0, z < groups - 1

    barrier = pltpu.get_barrier_semaphore()
    for partner in (sib, xn, yn):
        pl.semaphore_signal(barrier, inc=1, device_id=(z, partner), device_id_type=MESH)

    @pl.when(low)
    def _():
        pl.semaphore_signal(barrier, inc=1, device_id=(z - 1, col), device_id_type=MESH)

    @pl.when(high)
    def _():
        pl.semaphore_signal(barrier, inc=1, device_id=(z + 1, col), device_id_type=MESH)

    own_rows = table.at[:, pl.ds(col * rows, rows), :]
    fetch_i = pltpu.make_async_copy(integ, own_rows, local_sem.at[0])
    fetch_a = pltpu.make_async_copy(amp, own, local_sem.at[1])
    scalars = [
        pltpu.make_async_copy(src, dst, scalar_sem.at[i])
        for i, (src, dst) in enumerate(((source_hbm, source), (target_hbm, target), (mask_hbm, mask)))
    ]
    fetch_i.start()
    fetch_a.start()
    for scalar in scalars:
        scalar.start()
    pl.semaphore_wait(barrier, 3 + jnp.where(low, 1, 0) + jnp.where(high, 1, 0))

    tail = depth // TAIL_SHARE
    head = depth - tail
    chunk_rows = depth * 5 // 16
    starts = [chunk_rows * q for q in range(CHUNKS - 1)] + [head, depth]

    def piece(ref, q):
        if ref is None:
            if q == CHUNKS - 1:
                return far_tail
            ref = far_head
        return ref.at[:, pl.ds(starts[q], starts[q + 1] - starts[q]), :]

    ups, downs = (own, u1, u2, None), (own, d1, d2, None)

    def up(d, q):
        src = amp if d == 1 else ups[d - 1]
        i = (d - 1) * CHUNKS + q
        return pltpu.make_async_remote_copy(
            piece(src, q), piece(ups[d], q), usend.at[i], urecv.at[i],
            device_id=(z + 1, col), device_id_type=MESH)

    def down(d, q):
        src = amp if d == 1 else downs[d - 1]
        i = (d - 1) * CHUNKS + q
        return pltpu.make_async_remote_copy(
            piece(src, q), piece(downs[d], q), dsend.at[i], drecv.at[i],
            device_id=(z - 1, col), device_id_type=MESH)

    def rows_copy(i, block, first, count, partner):
        window = table.at[pl.ds(first, count), pl.ds(block * rows, rows), :]
        src = integ.at[pl.ds(first, count)] if i < 5 else window
        return pltpu.make_async_remote_copy(
            src, window, isend.at[i], irecv.at[i], device_id=(z, partner), device_id_type=MESH)

    moves = [
        rows_copy(0, col, 0, slots, sib),
        rows_copy(1, col, half, half, xn),
        rows_copy(2, col, 0, half, xn),
        rows_copy(3, col, 0, half, yn),
        rows_copy(4, col, half, half, yn),
        rows_copy(5, yn, 0, half, xn),
        rows_copy(6, xn, half, half, yn),
        rows_copy(7, xn, half, half, sib),
        rows_copy(8, xn, 0, half, sib),
        rows_copy(9, yn, 0, half, sib),
        rows_copy(10, yn, half, half, sib),
        rows_copy(11, diag, 0, half, sib),
        rows_copy(12, diag, half, half, sib),
    ]

    for q in range(CHUNKS):
        @pl.when(low)
        def _():
            down(1, q).start()

        @pl.when(high)
        def _():
            up(1, q).start()

    for i in (1, 3, 2, 4, 0):
        moves[i].start()

    def pass_on(d, q):
        @pl.when(z >= d)
        def _():
            up(d, q).wait_recv()
            if d < groups - 1:
                @pl.when(high)
                def _():
                    up(d + 1, q).start()

        @pl.when(z + d < groups)
        def _():
            down(d, q).wait_recv()
            if d < groups - 1:
                @pl.when(low)
                def _():
                    down(d + 1, q).start()

    out[...] = jnp.zeros_like(out)
    mid = CHUNKS // 2
    for q in range(mid):
        pass_on(1, q)
    moves[3].wait_recv()
    moves[5].start()
    moves[9].start()
    moves[1].wait_recv()
    moves[6].start()
    moves[7].start()
    for q in range(mid, CHUNKS):
        pass_on(1, q)
    moves[4].wait_recv()
    moves[10].start()
    moves[2].wait_recv()
    moves[8].start()
    for q in range(mid):
        pass_on(2, q)
    moves[5].wait_recv()
    moves[11].start()
    moves[6].wait_recv()
    moves[12].start()
    for q in range(mid, CHUNKS):
        pass_on(2, q)
    fetch_i.wait()
    fetch_a.wait()
    for i in (0, 7, 8, 9, 10, 11, 12):
        moves[i].wait_recv()

    for scalar in scalars:
        scalar.wait()

    def slots_of(group):
        first = jnp.int32(slots)
        last = jnp.int32(-1)
        for k in range(slots):
            match = source[k] // pairs == group
            first = jnp.where(match, jnp.minimum(first, k), first)
            last = jnp.where(match, jnp.maximum(last, k), last)
        found = []
        for k in (first, last):
            k = jnp.clip(k, 0, slots - 1)
            found.append((k, source[k] % pairs, jnp.where(mask[k] > 0, target[k], -1)))
        return found

    def contract(tiles, group):
        for k, tile, goal in slots_of(group):

            @pl.loop(0, depth // ROW_TILE)
            def _(r):
                span = pl.ds(pl.multiple_of(r * ROW_TILE, ROW_TILE), ROW_TILE)
                product = jnp.dot(table[k, span, :], tiles[tile], preferred_element_type=jnp.float32)
                product = product.astype(jnp.bfloat16).astype(jnp.float32)
                for p in range(pairs):
                    out[p, span, :] += jnp.where(goal == p, product, 0.0)

    contract(own, z)
    for d in range(1, groups - 1):
        @pl.when(z >= d)
        def _():
            contract(ups[d], z - d)

        @pl.when(z + d < groups)
        def _():
            contract(downs[d], z + d)

    last_hop = groups - 1
    for q in range(CHUNKS - 1):
        pass_on(last_hop, q)
    outer = (z == 0) | (z == groups - 1)

    @pl.when(outer)
    def _():
        for n, (k, tile, goal) in enumerate(slots_of(groups - 1 - z)):
            @pl.loop(0, depth // ROW_TILE)
            def _(r):
                span = pl.ds(pl.multiple_of(r * ROW_TILE, ROW_TILE), ROW_TILE)
                product = jnp.dot(table[k, span, :head], far_head[tile], preferred_element_type=jnp.float32)
                rest = table[k, span, head:]
                for p in range(pairs):
                    out[p, span, :] += jnp.where(goal == p, product, 0.0)
                    picked[p, span, n * tail:(n + 1) * tail] = jnp.where(goal == p, rest, jnp.zeros_like(rest))

    pass_on(last_hop, CHUNKS - 1)

    @pl.when(outer)
    def _():
        last_tiles = [far_tail[tile] for _, tile, _ in slots_of(groups - 1 - z)]
        rest = jnp.concatenate(last_tiles, axis=0)
        for p in range(pairs):
            for r in range(depth // ROW_TILE):
                span = slice(r * ROW_TILE, (r + 1) * ROW_TILE)
                out[p, span, :] += jnp.dot(picked[p, span, :], rest, preferred_element_type=jnp.float32)

    for move in moves:
        move.wait_send()
    for d in range(1, groups):
        for q in range(CHUNKS):
            @pl.when(high & (z >= d - 1))
            def _():
                up(d, q).wait_send()

            @pl.when(low & (z + d - 1 < groups))
            def _():
                down(d, q).wait_send()


def on_line(groups, amplitudes, integrals, source_pair, target_pair, symmetry_mask):
    pairs, depth, width = amplitudes.shape
    slots, rows, inner = integrals.shape
    across = depth // rows
    shard = pltpu.VMEM(amplitudes.shape, amplitudes.dtype)
    hops = (groups - 1) * CHUNKS
    return pl.pallas_call(
        functools.partial(line_kernel, groups),
        out_shape=pltpu.VMEM((pairs, depth, width), jnp.float32),
        in_specs=[pl.BlockSpec(memory_space=pltpu.HBM)] * 5,
        out_specs=pl.BlockSpec(memory_space=pltpu.VMEM),
        scratch_shapes=[
            pltpu.SMEM((slots,), jnp.int32),
            pltpu.SMEM((slots,), jnp.int32),
            pltpu.SMEM((slots,), jnp.int32),
            pltpu.VMEM((slots, rows * across, inner), integrals.dtype),
            shard, shard, shard, shard, shard,
            pltpu.VMEM((pairs, depth - depth // TAIL_SHARE, width), amplitudes.dtype),
            pltpu.VMEM((pairs, depth // TAIL_SHARE, width), amplitudes.dtype),
            pltpu.VMEM((pairs, depth, 2 * (depth // TAIL_SHARE)), integrals.dtype),
            pltpu.SemaphoreType.DMA((3,)),
            pltpu.SemaphoreType.DMA((2,)),
            pltpu.SemaphoreType.DMA((13,)),
            pltpu.SemaphoreType.DMA((13,)),
            pltpu.SemaphoreType.DMA((hops,)),
            pltpu.SemaphoreType.DMA((hops,)),
            pltpu.SemaphoreType.DMA((hops,)),
            pltpu.SemaphoreType.DMA((hops,)),
        ],
        compiler_params=pltpu.CompilerParams(
            collective_id=0, has_side_effects=True, vmem_limit_bytes=60 * 1024 * 1024
        ),
        cost_estimate=pl.CostEstimate(
            flops=2 * slots * depth * inner * width, bytes_accessed=16 * 1024 * 1024, transcendentals=0
        ),
    )(source_pair, target_pair, symmetry_mask, amplitudes, integrals)


def on_device(amplitudes, integrals, source_pair, target_pair, symmetry_mask):
    pairs = amplitudes.shape[0]
    tile_table = lax.all_gather(amplitudes, "row", axis=0, tiled=True)
    piece = lax.all_gather(integrals, "col", axis=1, tiled=True)
    total = [jnp.zeros(amplitudes.shape[1:], jnp.float32)] * pairs
    for slot in range(integrals.shape[0]):
        tile = lax.dynamic_index_in_dim(tile_table, source_pair[slot], 0, keepdims=False)
        product = jnp.dot(piece[slot], tile, preferred_element_type=jnp.float32).astype(jnp.bfloat16)
        goal = jnp.where(symmetry_mask[slot] > 0, target_pair[slot], -1)
        for p in range(pairs):
            total[p] += jnp.where(goal == p, product.astype(jnp.float32), 0.0)
    return jnp.stack(total)


def solution(mesh):
    placed = (P("row", None, "col"), P("row", "col", None), P("row"), P("row"), P("row"))
    groups = mesh.shape["row"]
    if groups == 4 and mesh.shape["col"] == 8:
        body = functools.partial(on_line, groups)
    else:
        body = on_device
    return jax.shard_map(
        body, mesh=mesh, in_specs=placed, out_specs=P("row", None, "col"), check_vma=False
    )
```

```python
import functools

import jax
import jax.numpy as jnp
from jax import lax
from jax.experimental import pallas as pl
from jax.experimental.pallas import tpu as pltpu
from jax.sharding import PartitionSpec as P

MESH = pl.DeviceIdType.MESH
CHUNKS = 4
ROW_TILE = 512


def line_kernel(groups, source_hbm, target_hbm, mask_hbm, amp, integ, out, source, target, mask, table, own,
                u1, u2, d1, d2, far_head, far_tail, part, scalar_sem,
                local_sem, isend, irecv, usend, urecv, dsend, drecv):
    z = lax.axis_index("row")
    col = lax.axis_index("col")
    core, x, y = col % 2, (col // 2) % 2, col // 4
    slots, rows, _ = integ.shape
    half = slots // 2
    pairs, depth, _ = amp.shape

    def place(py, px, pc):
        return (py * 2 + px) * 2 + pc

    sib, xn, yn = place(y, x, 1 - core), place(y, 1 - x, core), place(1 - y, x, core)
    diag = place(1 - y, 1 - x, core)
    low, high = z > 0, z < groups - 1

    barrier = pltpu.get_barrier_semaphore()
    for partner in (sib, xn, yn):
        pl.semaphore_signal(barrier, inc=1, device_id=(z, partner), device_id_type=MESH)

    @pl.when(low)
    def _():
        pl.semaphore_signal(barrier, inc=1, device_id=(z - 1, col), device_id_type=MESH)

    @pl.when(high)
    def _():
        pl.semaphore_signal(barrier, inc=1, device_id=(z + 1, col), device_id_type=MESH)

    own_rows = table.at[:, pl.ds(col * rows, rows), :]
    fetch_i = pltpu.make_async_copy(integ, own_rows, local_sem.at[0])
    fetch_a = pltpu.make_async_copy(amp, own, local_sem.at[1])
    scalars = [
        pltpu.make_async_copy(src, dst, scalar_sem.at[i])
        for i, (src, dst) in enumerate(((source_hbm, source), (target_hbm, target), (mask_hbm, mask)))
    ]
    fetch_i.start()
    fetch_a.start()
    for scalar in scalars:
        scalar.start()
    pl.semaphore_wait(barrier, 3 + jnp.where(low, 1, 0) + jnp.where(high, 1, 0))

    chunk_rows = depth // CHUNKS

    def piece(ref, q):
        if ref is None:
            if q == CHUNKS - 1:
                return far_tail
            ref = far_head
        return ref.at[:, pl.ds(q * chunk_rows, chunk_rows), :]

    ups, downs = (own, u1, u2, None), (own, d1, d2, None)

    def up(d, q):
        src = amp if d == 1 else ups[d - 1]
        i = (d - 1) * CHUNKS + q
        return pltpu.make_async_remote_copy(
            piece(src, q), piece(ups[d], q), usend.at[i], urecv.at[i],
            device_id=(z + 1, col), device_id_type=MESH)

    def down(d, q):
        src = amp if d == 1 else downs[d - 1]
        i = (d - 1) * CHUNKS + q
        return pltpu.make_async_remote_copy(
            piece(src, q), piece(downs[d], q), dsend.at[i], drecv.at[i],
            device_id=(z - 1, col), device_id_type=MESH)

    def rows_copy(i, block, first, count, partner):
        window = table.at[pl.ds(first, count), pl.ds(block * rows, rows), :]
        src = integ.at[pl.ds(first, count)] if i < 5 else window
        return pltpu.make_async_remote_copy(
            src, window, isend.at[i], irecv.at[i], device_id=(z, partner), device_id_type=MESH)

    moves = [
        rows_copy(0, col, 0, slots, sib),
        rows_copy(1, col, half, half, xn),
        rows_copy(2, col, 0, half, xn),
        rows_copy(3, col, 0, half, yn),
        rows_copy(4, col, half, half, yn),
        rows_copy(5, yn, 0, half, xn),
        rows_copy(6, xn, half, half, yn),
        rows_copy(7, xn, half, half, sib),
        rows_copy(8, xn, 0, half, sib),
        rows_copy(9, yn, 0, half, sib),
        rows_copy(10, yn, half, half, sib),
        rows_copy(11, diag, 0, half, sib),
        rows_copy(12, diag, half, half, sib),
    ]

    for q in range(CHUNKS):
        @pl.when(low)
        def _():
            down(1, q).start()

        @pl.when(high)
        def _():
            up(1, q).start()

    for i in (1, 3, 2, 4, 0):
        moves[i].start()

    def pass_on(d, q):
        @pl.when(z >= d)
        def _():
            up(d, q).wait_recv()
            if d < groups - 1:
                @pl.when(high)
                def _():
                    up(d + 1, q).start()

        @pl.when(z + d < groups)
        def _():
            down(d, q).wait_recv()
            if d < groups - 1:
                @pl.when(low)
                def _():
                    down(d + 1, q).start()

    out[...] = jnp.zeros_like(out)
    mid = CHUNKS // 2
    for q in range(mid):
        pass_on(1, q)
    moves[3].wait_recv()
    moves[5].start()
    moves[9].start()
    moves[1].wait_recv()
    moves[6].start()
    moves[7].start()
    for q in range(mid, CHUNKS):
        pass_on(1, q)
    moves[4].wait_recv()
    moves[10].start()
    moves[2].wait_recv()
    moves[8].start()
    for q in range(mid):
        pass_on(2, q)
    moves[5].wait_recv()
    moves[11].start()
    moves[6].wait_recv()
    moves[12].start()
    for q in range(mid, CHUNKS):
        pass_on(2, q)
    fetch_i.wait()
    fetch_a.wait()
    for i in (0, 7, 8, 9, 10, 11, 12):
        moves[i].wait_recv()

    for scalar in scalars:
        scalar.wait()

    def slots_of(group):
        first = jnp.int32(slots)
        last = jnp.int32(-1)
        for k in range(slots):
            match = source[k] // pairs == group
            first = jnp.where(match, jnp.minimum(first, k), first)
            last = jnp.where(match, jnp.maximum(last, k), last)
        found = []
        for k in (first, last):
            k = jnp.clip(k, 0, slots - 1)
            found.append((k, source[k] % pairs, jnp.where(mask[k] > 0, target[k], -1)))
        return found

    def contract(tiles, group):
        for k, tile, goal in slots_of(group):

            @pl.loop(0, depth // ROW_TILE)
            def _(r):
                span = pl.ds(pl.multiple_of(r * ROW_TILE, ROW_TILE), ROW_TILE)
                product = jnp.dot(table[k, span, :], tiles[tile], preferred_element_type=jnp.float32)
                product = product.astype(jnp.bfloat16).astype(jnp.float32)
                for p in range(pairs):
                    out[p, span, :] += jnp.where(goal == p, product, 0.0)

    contract(own, z)
    for d in range(1, groups - 1):
        @pl.when(z >= d)
        def _():
            contract(ups[d], z - d)

        @pl.when(z + d < groups)
        def _():
            contract(downs[d], z + d)

    last_hop = groups - 1
    for q in range(CHUNKS - 1):
        pass_on(last_hop, q)
    head = depth - chunk_rows
    outer = (z == 0) | (z == groups - 1)

    @pl.when(outer)
    def _():
        for n, (k, tile, _) in enumerate(slots_of(groups - 1 - z)):
            @pl.loop(0, depth // ROW_TILE)
            def _(r):
                span = pl.ds(pl.multiple_of(r * ROW_TILE, ROW_TILE), ROW_TILE)
                part[n, span, :] = jnp.dot(
                    table[k, span, :head], far_head[tile], preferred_element_type=jnp.float32)

    pass_on(last_hop, CHUNKS - 1)

    @pl.when(outer)
    def _():
        found = slots_of(groups - 1 - z)
        for r in range(depth // ROW_TILE):
            span = slice(r * ROW_TILE, (r + 1) * ROW_TILE)
            totals = [out[p, span, :] for p in range(pairs)]
            for n, (k, tile, goal) in enumerate(found):
                product = part[n, span, :] + jnp.dot(
                    table[k, span, head:], far_tail[tile], preferred_element_type=jnp.float32)
                product = product.astype(jnp.bfloat16).astype(jnp.float32)
                totals = [total + jnp.where(goal == p, product, 0.0) for p, total in enumerate(totals)]
            for p in range(pairs):
                out[p, span, :] = totals[p]

    for move in moves:
        move.wait_send()
    for d in range(1, groups):
        for q in range(CHUNKS):
            @pl.when(high & (z >= d - 1))
            def _():
                up(d, q).wait_send()

            @pl.when(low & (z + d - 1 < groups))
            def _():
                down(d, q).wait_send()


def on_line(groups, amplitudes, integrals, source_pair, target_pair, symmetry_mask):
    pairs, depth, width = amplitudes.shape
    slots, rows, inner = integrals.shape
    across = depth // rows
    shard = pltpu.VMEM(amplitudes.shape, amplitudes.dtype)
    hops = (groups - 1) * CHUNKS
    return pl.pallas_call(
        functools.partial(line_kernel, groups),
        out_shape=pltpu.VMEM((pairs, depth, width), jnp.float32),
        in_specs=[pl.BlockSpec(memory_space=pltpu.HBM)] * 5,
        out_specs=pl.BlockSpec(memory_space=pltpu.VMEM),
        scratch_shapes=[
            pltpu.SMEM((slots,), jnp.int32),
            pltpu.SMEM((slots,), jnp.int32),
            pltpu.SMEM((slots,), jnp.int32),
            pltpu.VMEM((slots, rows * across, inner), integrals.dtype),
            shard, shard, shard, shard, shard,
            pltpu.VMEM((pairs, depth - depth // CHUNKS, width), amplitudes.dtype),
            pltpu.VMEM((pairs, depth // CHUNKS, width), amplitudes.dtype),
            pltpu.VMEM((2, depth, width), jnp.float32),
            pltpu.SemaphoreType.DMA((3,)),
            pltpu.SemaphoreType.DMA((2,)),
            pltpu.SemaphoreType.DMA((13,)),
            pltpu.SemaphoreType.DMA((13,)),
            pltpu.SemaphoreType.DMA((hops,)),
            pltpu.SemaphoreType.DMA((hops,)),
            pltpu.SemaphoreType.DMA((hops,)),
            pltpu.SemaphoreType.DMA((hops,)),
        ],
        compiler_params=pltpu.CompilerParams(
            collective_id=0, has_side_effects=True, vmem_limit_bytes=60 * 1024 * 1024
        ),
        cost_estimate=pl.CostEstimate(
            flops=2 * slots * depth * inner * width, bytes_accessed=16 * 1024 * 1024, transcendentals=0
        ),
    )(source_pair, target_pair, symmetry_mask, amplitudes, integrals)


def on_device(amplitudes, integrals, source_pair, target_pair, symmetry_mask):
    pairs = amplitudes.shape[0]
    tile_table = lax.all_gather(amplitudes, "row", axis=0, tiled=True)
    piece = lax.all_gather(integrals, "col", axis=1, tiled=True)
    total = [jnp.zeros(amplitudes.shape[1:], jnp.float32)] * pairs
    for slot in range(integrals.shape[0]):
        tile = lax.dynamic_index_in_dim(tile_table, source_pair[slot], 0, keepdims=False)
        product = jnp.dot(piece[slot], tile, preferred_element_type=jnp.float32).astype(jnp.bfloat16)
        goal = jnp.where(symmetry_mask[slot] > 0, target_pair[slot], -1)
        for p in range(pairs):
            total[p] += jnp.where(goal == p, product.astype(jnp.float32), 0.0)
    return jnp.stack(total)


def solution(mesh):
    placed = (P("row", None, "col"), P("row", "col", None), P("row"), P("row"), P("row"))
    groups = mesh.shape["row"]
    if groups == 4 and mesh.shape["col"] == 8:
        body = functools.partial(on_line, groups)
    else:
        body = on_device
    return jax.shard_map(
        body, mesh=mesh, in_specs=placed, out_specs=P("row", None, "col"), check_vma=False
    )
```
